32 devices in a mesh: ga: 32 (over z, y, x, core), gp: 1.
Axes of the slice: x: 2, y: 2, z: 4, core: 2. Of those that a mesh axis runs over, the one named last changes fastest.
Arguments:
- screened: bfloat16 [8192, 65536], P('ga', 'gp'), may hold values from -0.0234375 to 0.0234375
- valence: bfloat16 [32, 32, 65536], P('ga', None, 'gp'), may hold values from -6 to 6
- conduction: bfloat16 [1024, 8192], P(None, 'ga'), may hold values from -0.125 to 0.125
- owner: int32 [6], replicated, may hold values from 0 to 31
Outputs:
- kernel: float32 [1024, 192], P('ga', 'gp')
The draws below stay inside these ranges and needn't reach their ends.
Inputs may be any that keep to these rules, and one draw needn't show every extreme that they name: owner[b] is the slot of valence, along its first dimension, that holds batch b.
All inputs are finite; a program needn't handle non-finite values.
Results may differ from the reference program's by a relative error of at most 0.0003.
Values may be sent and summed in bfloat16 or wider, within the bound.
A program may use at most 128 MiB of HBM per device.

```python
import jax
import jax.numpy as jnp
from jax import lax

NG = 65536
NV = 32
NC = 1024
NB = 6
GROWS = 8192
SLOTS = 32
N_GA = 32


def touch_ends(drawn, rng, smallest, largest):
    longest = drawn.shape.index(max(drawn.shape))
    spots = []
    for shift in (0, 1):
        where = [jax.random.randint(jax.random.fold_in(rng, axis), (), 0, length) for axis, length in enumerate(drawn.shape)]
        where[longest] = (where[longest] + shift) % drawn.shape[longest]
        spots.append(tuple(where))
    return drawn.at[spots[0]].set(smallest).at[spots[1]].set(largest)


def strengthened(drawn, rng, source, target, blocks, factor):
    def block_of(position):
        return (jnp.arange(drawn.shape[position]) // (drawn.shape[position] // blocks)).reshape((-1,) + (1,) * (drawn.ndim - 1 - position))

    one_side = jax.random.permutation(rng, blocks)[block_of(target)]
    second = (block_of(target) + blocks // 2) % blocks
    return jnp.where((block_of(source) == one_side) | (block_of(source) == second), factor * drawn, drawn)


def steps_of(own_key, dims, pieces, smallest, high):
    factor_of = 1.0
    for position, shards_of in pieces:
        draws = jax.random.uniform(jax.random.fold_in(jax.random.fold_in(own_key, 6), position), (shards_of,), jnp.float32, smallest / len(pieces), high / len(pieces))
        factor_of = factor_of * jnp.repeat(jnp.exp(draws), dims[position] // shards_of).reshape((-1,) + (1,) * (len(dims) - 1 - position))
    return factor_of


def gaussian(key, dims, width, most, pieces=(), dtype=jnp.bfloat16):
    entries = width * jax.random.normal(key, dims, jnp.float32)
    if pieces:
        entries = entries * steps_of(key, dims, pieces, -0.22, 0.18)
    return jnp.clip(entries, -most, most).astype(dtype)


def gaussian_with(own_key, dims, deviation, reach, cuts, heavy, kind=jnp.bfloat16):
    drawn = deviation * jax.random.normal(own_key, dims, jnp.float32)
    if cuts:
        drawn = drawn * steps_of(own_key, dims, cuts, -0.22, 0.18)
    return jnp.clip(strengthened(drawn, jax.random.fold_in(own_key, 3), *heavy), -reach, reach).astype(kind)


def setup_inputs(seed: int = 0) -> dict:
    key_list = jax.random.split(jax.random.key(seed), 5)
    screened = gaussian(key_list[0], (GROWS, NG), NG ** -0.5, 0.0234375, ((0, 32),))
    valence = gaussian(key_list[1], (SLOTS, NV, NG), 1.0, 6.0, ((0, 32),))
    conduction = gaussian_with(key_list[2], (NC, GROWS), GROWS ** -0.5, 0.125, ((1, 32),), (1, 0, 32, 2.75))
    owner = touch_ends(jax.random.randint(key_list[3], (NB,), 0, N_GA), jax.random.fold_in(key_list[3], 1), 0, N_GA - 1).astype(jnp.int32)
    return dict(screened=screened, valence=valence, conduction=conduction, owner=owner)


def reference(screened, valence, conduction, owner):
    chosen = valence[owner.astype(jnp.int32)]
    stacked = chosen.reshape(chosen.shape[0] * chosen.shape[1], chosen.shape[2])
    pair = lax.dot_general(screened, stacked, (((1,), (1,)), ((), ())), preferred_element_type=jnp.float32)
    kernel = jnp.dot(conduction.astype(jnp.float32), pair, precision=lax.Precision.HIGHEST)
    return kernel
```

```python
import functools

import jax
import jax.numpy as jnp
from jax import lax
from jax.experimental import pallas as pl
from jax.experimental.pallas import tpu as pltpu
from jax.sharding import PartitionSpec as P

WIDTH = 512
PLANE = 8
PLANES = 4
LAG = 2


def remote(src, dst, send, recv, target):
    copy = pltpu.make_async_remote_copy(
        src_ref=src, dst_ref=dst, send_sem=send, recv_sem=recv,
        device_id={"ga": target}, device_id_type=pl.DeviceIdType.MESH)
    copy.start()


def drain(ref, sem):
    pltpu.make_async_copy(ref, ref, sem).wait()


def kernel(chunks, weight, valence, screened, conduction, out,
           slots, own, below, above, chosen, panel, acc, term, sum_core, recv_core, recv_plane, sum_plane, recv_line,
           spread_send, spread_recv, up_send, up_recv, down_send, down_recv, gather_send, across_x, across_y, corner,
           partner_recv, panel_sem, core_sem, plane_send, plane_recv, line_send, line_recv):
    rows = chosen.shape[2]
    half = rows // 2
    nb = weight.shape[0]
    nv = valence.shape[0]
    me = lax.axis_index("ga")
    z = me // PLANE
    j = lax.rem(me, PLANE)
    y = j // 4
    x = lax.rem(j // 2, 2)
    c = lax.rem(j, 2)
    base = z * PLANE
    jx = y * 4 + (1 - x) * 2 + c
    jy = (1 - y) * 4 + x * 2 + c
    jd = (1 - y) * 4 + (1 - x) * 2 + c
    jp = y * 4 + x * 2 + (1 - c)

    barrier = pltpu.get_barrier_semaphore()
    for step in range(1, PLANE):
        pl.semaphore_signal(barrier, inc=1, device_id={"ga": base + lax.rem(j + step, PLANE)}, device_id_type=pl.DeviceIdType.MESH)
    for step in range(1, PLANES):
        pl.semaphore_signal(barrier, inc=1, device_id={"ga": lax.rem(z + step, PLANES) * PLANE + j}, device_id_type=pl.DeviceIdType.MESH)
    pl.semaphore_wait(barrier, PLANE + PLANES - 2)

    def columns(t, piece):
        return pl.ds(pl.multiple_of((t * PLANE + piece) * WIDTH, WIDTH), WIDTH)

    def load_panel(t):
        wide = pl.ds(pl.multiple_of(t * PLANE * WIDTH, WIDTH), PLANE * WIDTH)
        slot = lax.rem(t, 2)
        return pltpu.make_async_copy(screened.at[:, wide], panel.at[slot], panel_sem.at[slot])

    def spread(t, carry):
        pltpu.make_async_copy(valence.at[:, columns(t, j)], slots.at[t, j], spread_recv.at[t]).start()
        for step in range(1, PLANE):
            piece = lax.rem(j + step, PLANE)
            remote(valence.at[:, columns(t, piece)], slots.at[t, j], spread_send.at[t], spread_recv.at[t], base + piece)
        return carry

    lax.fori_loop(0, chunks, spread, 0)
    load_panel(0).start()
    load_panel(1).start()
    acc[...] = jnp.zeros_like(acc)

    def pick(t):
        drain(slots.at[t], spread_recv.at[t])
        for b in range(nb):
            value = weight[b, 0] * slots[t, 0].astype(jnp.float32)
            for s in range(1, PLANE):
                value += weight[b, s] * slots[t, s].astype(jnp.float32)
            own[t, b * nv:(b + 1) * nv, :] = value.astype(jnp.bfloat16)

        @pl.when(z == 0)
        def _():
            remote(own.at[t], below.at[t], up_send.at[t], up_recv.at[t], me + PLANE)

        @pl.when(z == PLANES - 1)
        def _():
            remote(own.at[t], above.at[t], down_send.at[t], down_recv.at[t], me - PLANE)

        @pl.when(z == 1)
        def _():
            drain(below.at[t], up_recv.at[t])
            below[t] = below[t] + own[t]
            remote(below.at[t], below.at[t], up_send.at[t], up_recv.at[t], me + PLANE)

        @pl.when(z == 2)
        def _():
            drain(above.at[t], down_recv.at[t])
            above[t] = above[t] + own[t]
            remote(above.at[t], above.at[t], down_send.at[t], down_recv.at[t], me - PLANE)

    def total(t):
        @pl.when(z == 0)
        def _():
            drain(above.at[t], down_recv.at[t])
            chosen[t, j] = own[t] + above[t]

        @pl.when(z == PLANES - 1)
        def _():
            drain(below.at[t], up_recv.at[t])
            chosen[t, j] = own[t] + below[t]

        @pl.when(z == 1)
        def _():
            drain(above.at[t], down_recv.at[t])
            chosen[t, j] = below[t] + above[t]
            above[t] = above[t] + own[t]
            remote(above.at[t], above.at[t], down_send.at[t], down_recv.at[t], me - PLANE)

        @pl.when(z == 2)
        def _():
            drain(below.at[t], up_recv.at[t])
            chosen[t, j] = below[t] + above[t]
            below[t] = below[t] + own[t]
            remote(below.at[t], below.at[t], up_send.at[t], up_recv.at[t], me + PLANE)

        block = chosen.at[t, j]
        remote(block, block, gather_send.at[t], across_x.at[t], base + jx)
        remote(block, block, gather_send.at[t], across_y.at[t], base + jy)
        remote(block, block, gather_send.at[t], partner_recv.at[t], base + jp)

    def relay(t):
        drain(chosen.at[t, jx], across_x.at[t])
        late = chosen.at[t, jx, pl.ds(half, half)]
        remote(late, late, gather_send.at[t], corner.at[t], base + jy)
        drain(chosen.at[t, jy], across_y.at[t])
        early = chosen.at[t, jy, pl.ds(0, half)]
        remote(early, early, gather_send.at[t], corner.at[t], base + jx)
        for piece in (jx, jy):
            block = chosen.at[t, piece]
            remote(block, block, gather_send.at[t], partner_recv.at[t], base + jp)

    def last(t):
        drain(chosen.at[t, jd], corner.at[t])
        block = chosen.at[t, jd]
        remote(block, block, gather_send.at[t], partner_recv.at[t], base + jp)

    dims = (((1,), (1,)), ((), ()))

    def multiply(t):
        drain(chosen.at[t, pl.ds(0, 4)], partner_recv.at[t])
        load_panel(t).wait()
        slot = lax.rem(t, 2)
        value = acc[...]
        for piece in range(PLANE):
            value += lax.dot_general(panel[slot, :, piece * WIDTH:(piece + 1) * WIDTH], chosen[t, piece], dims,
                                     preferred_element_type=jnp.float32)
        acc[...] = value

        @pl.when(t + 2 < chunks)
        def _():
            load_panel(t + 2).start()

    shift = jnp.where((z == 0) | (z == PLANES - 1), 2, 0)

    def stage(t, action):
        @pl.when((t >= 0) & (t < chunks))
        def _():
            action(t)

    def turn(t, carry):
        stage(t, pick)
        u = t - LAG - shift
        stage(u, total)
        stage(u - LAG, relay)
        stage(u - 2 * LAG, last)
        stage(u - 3 * LAG, multiply)
        return carry

    lax.fori_loop(0, chunks + 4 * LAG + 2, turn, 0)

    value = acc[...]
    high = value.astype(jnp.bfloat16)
    rest = value - high.astype(jnp.float32)
    middle = rest.astype(jnp.bfloat16)
    low = (rest - middle.astype(jnp.float32)).astype(jnp.bfloat16)
    group = term.shape[2]
    per = 2 * group
    for k in range(term.shape[0]):
        left = conduction[k * per:(k + 1) * per, :]
        block = jnp.dot(left, low, preferred_element_type=jnp.float32)
        block += jnp.dot(left, middle, preferred_element_type=jnp.float32)
        block += jnp.dot(left, high, preferred_element_type=jnp.float32)
        term[k, 0] = block[:group]
        term[k, 1] = block[group:]

    remote(term.at[:, 1 - c], recv_core, core_sem.at[0], core_sem.at[1], base + jp)
    drain(recv_core, core_sem.at[1])
    for k in range(term.shape[0]):
        sum_core[k // 4, k % 4] = term[k, c] + recv_core[k]

    flips = (y * 2 + 1 - x, (1 - y) * 2 + x, (1 - y) * 2 + 1 - x)
    for r, chip in enumerate(flips):
        remote(sum_core.at[:, chip], recv_plane.at[r], plane_send.at[r], plane_recv.at[r], base + chip * 2 + c)
    for r in range(3):
        drain(recv_plane.at[r], plane_recv.at[r])
    mine = y * 2 + x
    for k in range(PLANES):
        sum_plane[k] = (sum_core[k, mine] + recv_plane[0, k]) + (recv_plane[1, k] + recv_plane[2, k])

    for d in range(1, PLANES):
        other = lax.rem(z + d, PLANES)
        remote(sum_plane.at[other], recv_line.at[d - 1], line_send.at[d - 1], line_recv.at[d - 1], other * PLANE + j)
    for d in range(PLANES - 1):
        drain(recv_line.at[d], line_recv.at[d])
    out[...] = (sum_plane[z] + recv_line[0]) + (recv_line[1] + recv_line[2])

    drain(recv_core, core_sem.at[0])
    for r in range(3):
        drain(recv_plane.at[r], plane_send.at[r])
        drain(recv_line.at[r], line_send.at[r])

    def finish(t, carry):
        drain(slots.at[t, pl.ds(0, PLANE - 1)], spread_send.at[t])
        drain(chosen.at[t, pl.ds(0, PLANE - 1)], gather_send.at[t])

        @pl.when(z < PLANES - 1)
        def _():
            drain(below.at[t], up_send.at[t])

        @pl.when(z > 0)
        def _():
            drain(above.at[t], down_send.at[t])

        return carry

    lax.fori_loop(0, chunks, finish, 0)


def fused(screened, valence, conduction, owner):
    own_slot = valence[0]
    nv, ng = own_slot.shape
    nb = owner.shape[0]
    rows = nb * nv
    chunks = ng // (PLANE * WIDTH)
    nc = conduction.shape[0]
    mine = nc // (PLANE * PLANES)
    plane = lax.axis_index("ga") // PLANE
    weight = (owner[:, None] == plane * PLANE + jnp.arange(PLANE)[None, :]).astype(jnp.float32)
    bf16, f32 = jnp.bfloat16, jnp.float32
    dma = pltpu.SemaphoreType.DMA
    line = pltpu.VMEM((chunks, rows, WIDTH), bf16)
    vmem = pl.BlockSpec(memory_space=pltpu.VMEM)
    anyspace = pl.BlockSpec(memory_space=pl.ANY)
    return pl.pallas_call(
        functools.partial(kernel, chunks),
        out_shape=jax.ShapeDtypeStruct((mine, rows), f32),
        in_specs=[pl.BlockSpec(memory_space=pltpu.SMEM), anyspace, anyspace, vmem],
        out_specs=vmem,
        scratch_shapes=[
            pltpu.VMEM((chunks, PLANE, nv, WIDTH), bf16),
            line, line, line,
            pltpu.VMEM((chunks, PLANE, rows, WIDTH), bf16),
            pltpu.VMEM((2, screened.shape[0], PLANE * WIDTH), bf16),
            pltpu.VMEM((screened.shape[0], rows), f32),
            pltpu.VMEM((PLANE * PLANES // 2, 2, mine, rows), f32),
            pltpu.VMEM((PLANES, 4, mine, rows), f32),
            pltpu.VMEM((PLANE * PLANES // 2, mine, rows), f32),
            pltpu.VMEM((3, PLANES, mine, rows), f32),
            pltpu.VMEM((PLANES, mine, rows), f32),
            pltpu.VMEM((3, mine, rows), f32),
        ] + [dma((chunks,))] * 11 + [dma((2,))] * 2 + [dma((3,))] * 4,
        compiler_params=pltpu.CompilerParams(collective_id=0, has_side_effects=True, vmem_limit_bytes=58 * 2**20),
        cost_estimate=pl.CostEstimate(flops=2 * screened.shape[0] * ng * rows, bytes_accessed=2 * screened.size, transcendentals=0),
    )(weight, own_slot, screened, conduction)


def spread_batch(block, axis, source):
    block = jnp.where(lax.axis_index(axis) == source, block, jnp.zeros_like(block))
    return lax.psum(block, axis)


def general(screened, valence, conduction, owner):
    own_slot = valence[0]
    dims = (((1,), (1,)), ((), ()))
    pieces = []
    for batch in range(owner.shape[0]):
        chosen = spread_batch(own_slot, "ga", owner[batch])
        pieces.append(lax.dot_general(screened, chosen, dims, preferred_element_type=jnp.float32))
    partial_value = jnp.concatenate(pieces, axis=1)
    cond_full = conduction.astype(jnp.float32)
    term = jnp.dot(cond_full, partial_value, precision=lax.Precision.HIGHEST)
    columns = lax.psum_scatter(term, "gp", scatter_dimension=1, tiled=True)
    return lax.psum_scatter(columns, "ga", scatter_dimension=0, tiled=True)


def solution(mesh):
    placed = (P("ga", "gp"), P("ga", None, "gp"), P(None, "ga"), P())
    body = fused if mesh.shape["ga"] == PLANE * PLANES and mesh.shape["gp"] == 1 else general
    return jax.shard_map(body, mesh=mesh, in_specs=placed, out_specs=P("ga", "gp"), check_vma=False)
```

```python
import functools

import jax
import jax.numpy as jnp
from jax import lax
from jax.experimental import pallas as pl
from jax.experimental.pallas import tpu as pltpu
from jax.sharding import PartitionSpec as P

WIDTH = 512
PLANE = 8
PLANES = 4
LAG = 2


def remote(src, dst, send, recv, target):
    copy = pltpu.make_async_remote_copy(
        src_ref=src, dst_ref=dst, send_sem=send, recv_sem=recv,
        device_id={"ga": target}, device_id_type=pl.DeviceIdType.MESH)
    copy.start()


def drain(ref, sem):
    pltpu.make_async_copy(ref, ref, sem).wait()


def kernel(chunks, weight, valence, screened, conduction, out,
           slots, own, below, above, chosen, panel, acc, term, sum_core, recv_core, recv_plane, sum_plane, recv_line,
           spread_send, spread_recv, up_send, up_recv, down_send, down_recv, gather_send, across_x, across_y, corner,
           pair_recv, partner_recv, panel_sem, core_sem, plane_send, plane_recv, line_send, line_recv):
    rows = chosen.shape[2]
    half = rows // 2
    quarter = half // 2
    nb = weight.shape[0]
    nv = valence.shape[0]
    me = lax.axis_index("ga")
    z = me // PLANE
    j = lax.rem(me, PLANE)
    y = j // 4
    x = lax.rem(j // 2, 2)
    c = lax.rem(j, 2)
    base = z * PLANE
    jx = y * 4 + (1 - x) * 2 + c
    jy = (1 - y) * 4 + x * 2 + c
    jd = (1 - y) * 4 + (1 - x) * 2 + c
    jp = y * 4 + x * 2 + (1 - c)
    odd = lax.rem(z, 2)
    first = odd * half
    pair = me + PLANE - 2 * PLANE * odd

    barrier = pltpu.get_barrier_semaphore()
    for step in range(1, PLANE):
        pl.semaphore_signal(barrier, inc=1, device_id={"ga": base + lax.rem(j + step, PLANE)}, device_id_type=pl.DeviceIdType.MESH)
    for step in range(1, PLANES):
        pl.semaphore_signal(barrier, inc=1, device_id={"ga": lax.rem(z + step, PLANES) * PLANE + j}, device_id_type=pl.DeviceIdType.MESH)
    pl.semaphore_wait(barrier, PLANE + PLANES - 2)

    def columns(t, piece):
        return pl.ds(pl.multiple_of((t * PLANE + piece) * WIDTH, WIDTH), WIDTH)

    def load_panel(t):
        wide = pl.ds(pl.multiple_of(t * PLANE * WIDTH, WIDTH), PLANE * WIDTH)
        slot = lax.rem(t, 2)
        return pltpu.make_async_copy(screened.at[:, wide], panel.at[slot], panel_sem.at[slot])

    def spread(t, carry):
        pltpu.make_async_copy(valence.at[:, columns(t, j)], slots.at[t, j], spread_recv.at[t]).start()
        for step in range(1, PLANE):
            piece = lax.rem(j + step, PLANE)
            remote(valence.at[:, columns(t, piece)], slots.at[t, j], spread_send.at[t], spread_recv.at[t], base + piece)
        return carry

    lax.fori_loop(0, chunks, spread, 0)
    load_panel(0).start()
    load_panel(1).start()
    acc[...] = jnp.zeros_like(acc)

    def pick(t):
        drain(slots.at[t], spread_recv.at[t])
        for b in range(nb):
            value = weight[b, 0] * slots[t, 0].astype(jnp.float32)
            for s in range(1, PLANE):
                value += weight[b, s] * slots[t, s].astype(jnp.float32)
            own[t, b * nv:(b + 1) * nv, :] = value.astype(jnp.bfloat16)

        @pl.when(z == 0)
        def _():
            remote(own.at[t], below.at[t], up_send.at[t], up_recv.at[t], me + PLANE)

        @pl.when(z == PLANES - 1)
        def _():
            remote(own.at[t], above.at[t], down_send.at[t], down_recv.at[t], me - PLANE)

        @pl.when(z == 1)
        def _():
            drain(below.at[t], up_recv.at[t])
            below[t] = below[t] + own[t]
            remote(below.at[t], below.at[t], up_send.at[t], up_recv.at[t], me + PLANE)

        @pl.when(z == 2)
        def _():
            drain(above.at[t], down_recv.at[t])
            above[t] = above[t] + own[t]
            remote(above.at[t], above.at[t], down_send.at[t], down_recv.at[t], me - PLANE)

    def total(t):
        @pl.when(z == 0)
        def _():
            drain(above.at[t], down_recv.at[t])
            chosen[t, j] = own[t] + above[t]

        @pl.when(z == PLANES - 1)
        def _():
            drain(below.at[t], up_recv.at[t])
            chosen[t, j] = own[t] + below[t]

        @pl.when(z == 1)
        def _():
            drain(above.at[t], down_recv.at[t])
            chosen[t, j] = below[t] + above[t]
            above[t] = above[t] + own[t]
            remote(above.at[t], above.at[t], down_send.at[t], down_recv.at[t], me - PLANE)

        @pl.when(z == 2)
        def _():
            drain(below.at[t], up_recv.at[t])
            chosen[t, j] = below[t] + above[t]
            below[t] = below[t] + own[t]
            remote(below.at[t], below.at[t], up_send.at[t], up_recv.at[t], me + PLANE)

        block = chosen.at[t, j]
        remote(block, block, gather_send.at[t], across_x.at[t], base + jx)
        remote(block, block, gather_send.at[t], across_y.at[t], base + jy)
        remote(block, block, gather_send.at[t], partner_recv.at[t], base + jp)

    def relay(t):
        drain(chosen.at[t, jx], across_x.at[t])
        late = chosen.at[t, jx, pl.ds(pl.multiple_of(first + quarter, 16), quarter)]
        remote(late, late, gather_send.at[t], corner.at[t], base + jy)
        drain(chosen.at[t, jy], across_y.at[t])
        early = chosen.at[t, jy, pl.ds(pl.multiple_of(first, 16), quarter)]
        remote(early, early, gather_send.at[t], corner.at[t], base + jx)
        for piece in (jx, jy):
            block = chosen.at[t, piece]
            remote(block, block, gather_send.at[t], partner_recv.at[t], base + jp)

    def swap(t):
        drain(chosen.at[t, jd, pl.ds(0, half)], corner.at[t])
        share = chosen.at[t, jd, pl.ds(pl.multiple_of(first, 16), half)]
        remote(share, share, gather_send.at[t], pair_recv.at[t], pair)

    def last(t):
        drain(chosen.at[t, jd, pl.ds(0, half)], pair_recv.at[t])
        block = chosen.at[t, jd]
        remote(block, block, gather_send.at[t], partner_recv.at[t], base + jp)

    dims = (((1,), (1,)), ((), ()))

    def multiply(t):
        drain(chosen.at[t, pl.ds(0, 4)], partner_recv.at[t])
        load_panel(t).wait()
        slot = lax.rem(t, 2)
        value = acc[...]
        for piece in range(PLANE):
            value += lax.dot_general(panel[slot, :, piece * WIDTH:(piece + 1) * WIDTH], chosen[t, piece], dims,
                                     preferred_element_type=jnp.float32)
        acc[...] = value

        @pl.when(t + 2 < chunks)
        def _():
            load_panel(t + 2).start()

    shift = jnp.where((z == 0) | (z == PLANES - 1), 2, 0)

    def stage(t, action):
        @pl.when((t >= 0) & (t < chunks))
        def _():
            action(t)

    def turn(t, carry):
        stage(t, pick)
        u = t - LAG - shift
        stage(u, total)
        stage(u - LAG, relay)
        stage(u - 2 * LAG, swap)
        stage(u - 4 * LAG, last)
        stage(u - 5 * LAG, multiply)
        return carry

    lax.fori_loop(0, chunks + 6 * LAG + 2, turn, 0)

    value = acc[...]
    high = value.astype(jnp.bfloat16)
    rest = value - high.astype(jnp.float32)
    middle = rest.astype(jnp.bfloat16)
    low = (rest - middle.astype(jnp.float32)).astype(jnp.bfloat16)
    group = term.shape[2]
    per = 2 * group
    for k in range(term.shape[0]):
        left = conduction[k * per:(k + 1) * per, :]
        block = jnp.dot(left, low, preferred_element_type=jnp.float32)
        block += jnp.dot(left, middle, preferred_element_type=jnp.float32)
        block += jnp.dot(left, high, preferred_element_type=jnp.float32)
        term[k, 0] = block[:group]
        term[k, 1] = block[group:]

    remote(term.at[:, 1 - c], recv_core, core_sem.at[0], core_sem.at[1], base + jp)
    drain(recv_core, core_sem.at[1])
    for k in range(term.shape[0]):
        sum_core[k // 4, k % 4] = term[k, c] + recv_core[k]

    flips = (y * 2 + 1 - x, (1 - y) * 2 + x, (1 - y) * 2 + 1 - x)
    for r, chip in enumerate(flips):
        remote(sum_core.at[:, chip], recv_plane.at[r], plane_send.at[r], plane_recv.at[r], base + chip * 2 + c)
    for r in range(3):
        drain(recv_plane.at[r], plane_recv.at[r])
    mine = y * 2 + x
    for k in range(PLANES):
        sum_plane[k] = (sum_core[k, mine] + recv_plane[0, k]) + (recv_plane[1, k] + recv_plane[2, k])

    for d in range(1, PLANES):
        other = lax.rem(z + d, PLANES)
        remote(sum_plane.at[other], recv_line.at[d - 1], line_send.at[d - 1], line_recv.at[d - 1], other * PLANE + j)
    for d in range(PLANES - 1):
        drain(recv_line.at[d], line_recv.at[d])
    out[...] = (sum_plane[z] + recv_line[0]) + (recv_line[1] + recv_line[2])

    drain(recv_core, core_sem.at[0])
    for r in range(3):
        drain(recv_plane.at[r], plane_send.at[r])
        drain(recv_line.at[r], line_send.at[r])

    def finish(t, carry):
        drain(slots.at[t, pl.ds(0, PLANE - 1)], spread_send.at[t])
        drain(chosen.at[t, pl.ds(0, PLANE - 1)], gather_send.at[t])

        @pl.when(z < PLANES - 1)
        def _():
            drain(below.at[t], up_send.at[t])

        @pl.when(z > 0)
        def _():
            drain(above.at[t], down_send.at[t])

        return carry

    lax.fori_loop(0, chunks, finish, 0)


def fused(screened, valence, conduction, owner):
    own_slot = valence[0]
    nv, ng = own_slot.shape
    nb = owner.shape[0]
    rows = nb * nv
    chunks = ng // (PLANE * WIDTH)
    nc = conduction.shape[0]
    mine = nc // (PLANE * PLANES)
    plane = lax.axis_index("ga") // PLANE
    weight = (owner[:, None] == plane * PLANE + jnp.arange(PLANE)[None, :]).astype(jnp.float32)
    bf16, f32 = jnp.bfloat16, jnp.float32
    dma = pltpu.SemaphoreType.DMA
    line = pltpu.VMEM((chunks, rows, WIDTH), bf16)
    vmem = pl.BlockSpec(memory_space=pltpu.VMEM)
    anyspace = pl.BlockSpec(memory_space=pl.ANY)
    return pl.pallas_call(
        functools.partial(kernel, chunks),
        out_shape=jax.ShapeDtypeStruct((mine, rows), f32),
        in_specs=[pl.BlockSpec(memory_space=pltpu.SMEM), anyspace, anyspace, vmem],
        out_specs=vmem,
        scratch_shapes=[
            pltpu.VMEM((chunks, PLANE, nv, WIDTH), bf16),
            line, line, line,
            pltpu.VMEM((chunks, PLANE, rows, WIDTH), bf16),
            pltpu.VMEM((2, screened.shape[0], PLANE * WIDTH), bf16),
            pltpu.VMEM((screened.shape[0], rows), f32),
            pltpu.VMEM((PLANE * PLANES // 2, 2, mine, rows), f32),
            pltpu.VMEM((PLANES, 4, mine, rows), f32),
            pltpu.VMEM((PLANE * PLANES // 2, mine, rows), f32),
            pltpu.VMEM((3, PLANES, mine, rows), f32),
            pltpu.VMEM((PLANES, mine, rows), f32),
            pltpu.VMEM((3, mine, rows), f32),
        ] + [dma((chunks,))] * 12 + [dma((2,))] * 2 + [dma((3,))] * 4,
        compiler_params=pltpu.CompilerParams(collective_id=0, has_side_effects=True, vmem_limit_bytes=58 * 2**20),
        cost_estimate=pl.CostEstimate(flops=2 * screened.shape[0] * ng * rows, bytes_accessed=2 * screened.size, transcendentals=0),
    )(weight, own_slot, screened, conduction)


def spread_batch(block, axis, source):
    block = jnp.where(lax.axis_index(axis) == source, block, jnp.zeros_like(block))
    return lax.psum(block, axis)


def general(screened, valence, conduction, owner):
    own_slot = valence[0]
    dims = (((1,), (1,)), ((), ()))
    pieces = []
    for batch in range(owner.shape[0]):
        chosen = spread_batch(own_slot, "ga", owner[batch])
        pieces.append(lax.dot_general(screened, chosen, dims, preferred_element_type=jnp.float32))
    partial_value = jnp.concatenate(pieces, axis=1)
    cond_full = conduction.astype(jnp.float32)
    term = jnp.dot(cond_full, partial_value, precision=lax.Precision.HIGHEST)
    columns = lax.psum_scatter(term, "gp", scatter_dimension=1, tiled=True)
    return lax.psum_scatter(columns, "ga", scatter_dimension=0, tiled=True)


def solution(mesh):
    placed = (P("ga", "gp"), P("ga", None, "gp"), P(None, "ga"), P())
    body = fused if mesh.shape["ga"] == PLANE * PLANES and mesh.shape["gp"] == 1 else general
    return jax.shard_map(body, mesh=mesh, in_specs=placed, out_specs=P("ga", "gp"), check_vma=False)
```
